32 devices in a mesh: loop: 8 (over z, core), grp: 4 (over y, x).
Axes of the slice: x: 2, y: 2, z: 4, core: 2. Of those that a mesh axis runs over, the one named last changes fastest.
Arguments:
- node_feats: bfloat16 [512, 8192], P(None, ('loop', 'grp')), may hold values from -6 to 6
- tile_vals: bfloat16 [8, 8, 10, 128, 128], P('loop'), may hold values from -0.375 to 0.375
- tile_rows: int32 [8, 8, 10], P('loop'), may hold values from 0 to 7
- tile_cols: int32 [8, 8, 10], P('loop'), may hold values from 0 to 7
- tile_count: int32 [8, 8], P('loop'), may hold values from 0 to 10, as said below
- degree: int32 [8192], P('loop'), may hold values from 1 to 8
- w_self: bfloat16 [512, 512], replicated, may hold values from -0.25 to 0.25
- w_neigh: bfloat16 [512, 512], replicated, may hold values from -0.25 to 0.25
Outputs:
- node_out: bfloat16 [512, 8192], P(None, ('loop', 'grp'))
The draws below stay inside these ranges and needn't reach their ends.
Inputs may be any that keep to these rules, and one draw needn't show every extreme that they name: Only the first tile_count[j, t] slots of a pair are tiles of the graph; later slots hold values that belong to no edge. Some pair uses all 10 slots in every draw.
All inputs are finite; a program needn't handle non-finite values.
Results may differ from the reference program's by a relative error of at most 0.0035.
Values may be sent and summed in bfloat16 or wider, within the bound.
A program may use at most 64 MiB of HBM per device.

```python
import jax
import jax.numpy as jnp
from jax import lax

F = 512
TB = 128
CAP = 10
SET = 1024
BLOCKS = 8
NODES = 8192
N_LOOP = 8


def draw_tile_count(key, part):
    sample_one = jax.random.randint(jax.random.fold_in(key, 11), (N_LOOP, N_LOOP), 0, CAP + 1)
    sample_two = jax.random.randint(jax.random.fold_in(key, 12), (N_LOOP, N_LOOP), 0, CAP + 1)
    counts = jnp.maximum(sample_one, sample_two)
    source_pick = jax.random.randint(jax.random.fold_in(key, 13), (), 0, N_LOOP)
    target_pick = jax.random.randint(jax.random.fold_in(key, 14), (), 0, N_LOOP)
    counts = counts.at[source_pick, target_pick].set(CAP)
    return counts.astype(jnp.int32)


def plant(array, stream_key, low, top_value):
    longest = array.shape.index(max(array.shape))
    spots = []
    for shift in (0, 1):
        where = [jax.random.randint(jax.random.fold_in(stream_key, axis), (), 0, length) for axis, length in enumerate(array.shape)]
        where[longest] = (where[longest] + shift) % array.shape[longest]
        spots.append(tuple(where))
    return array.at[spots[0]].set(low).at[spots[1]].set(top_value)


def shard_levels(stream_key, shape, shards, low, top_value):
    loudness, own = 1.0, jax.random.fold_in(stream_key, 6)
    for axis_at, blocks in shards:
        draws = jnp.exp(jax.random.uniform(jax.random.fold_in(own, axis_at), (blocks,), jnp.float32, low / len(shards), top_value / len(shards)))
        loudness = loudness * jnp.repeat(draws, shape[axis_at] // blocks).reshape([-1 if axis == axis_at else 1 for axis in range(len(shape))])
    return loudness


def scatter_about(stream_key, extent, scale, reach, cuts=(), held_as=jnp.bfloat16):
    array = jax.random.normal(stream_key, extent, jnp.float32) * scale
    if len(cuts) > 0:
        array = shard_levels(stream_key, extent, cuts, -0.22, 0.18) * array
    return jnp.clip(array, min=-reach, max=reach).astype(held_as)


def setup_inputs(seed: int = 0) -> dict:
    seeds = jax.random.split(jax.random.key(seed), 9)
    return {
        "node_feats": scatter_about(seeds[0], (F, NODES), 1.0, 6.0, ((1, 32),)),
        "tile_vals": scatter_about(seeds[1], (N_LOOP, N_LOOP, CAP, TB, TB), (2 * TB) ** -0.5, 0.375, ((0, 8),)),
        "tile_rows": plant(jax.random.randint(seeds[2], (N_LOOP, N_LOOP, CAP), 0, BLOCKS), jax.random.fold_in(seeds[2], 1), 0, BLOCKS - 1).astype(jnp.int32),
        "tile_cols": plant(jax.random.randint(seeds[3], (N_LOOP, N_LOOP, CAP), 0, BLOCKS), jax.random.fold_in(seeds[3], 1), 0, BLOCKS - 1).astype(jnp.int32),
        "tile_count": draw_tile_count(jax.random.fold_in(seeds[8], 71), 0),
        "degree": plant(jax.random.randint(seeds[5], (NODES,), 1, 9), jax.random.fold_in(seeds[5], 1), 1, 8).astype(jnp.int32),
        "w_self": scatter_about(seeds[6], (F, F), F ** -0.5, 0.25),
        "w_neigh": scatter_about(seeds[7], (F, F), F ** -0.5, 0.25),
    }


def contribute(sources, tiles, row_ids, col_ids, filled):
    grouped = sources.reshape(F, BLOCKS, TB)
    chosen = jnp.take(grouped, col_ids, axis=1)
    products = jnp.einsum('fkc,krc->kfr', chosen.astype(jnp.float32), tiles.astype(jnp.float32))
    active = jnp.arange(CAP, dtype=jnp.int32) < filled
    placer = ((row_ids[:, None] == jnp.arange(BLOCKS, dtype=jnp.int32)[None, :]) & active[:, None]).astype(jnp.float32)
    spread = jnp.einsum('kb,kfr->fbr', placer, products, precision=lax.Precision.HIGHEST)
    return spread.reshape(F, SET)

def reference(node_feats, tile_vals, tile_rows, tile_cols, tile_count, degree, w_self, w_neigh):

    def for_target(target):

        def accumulate(running, source):
            sources = lax.dynamic_slice_in_dim(node_feats, (source * SET).astype(jnp.int32), SET, 1)
            added = contribute(sources, tile_vals[source, target], tile_rows[source, target], tile_cols[source, target], tile_count[source, target])
            return (running + added, None)
        running, _ = lax.scan(accumulate, jnp.zeros((F, SET), jnp.float32), jnp.arange(N_LOOP, dtype=jnp.int32))
        return running
    per_set = lax.map(for_target, jnp.arange(N_LOOP, dtype=jnp.int32))
    summed = jnp.transpose(per_set, (1, 0, 2)).reshape(F, NODES)
    neigh = (summed / degree.astype(jnp.float32)[None, :]).astype(jnp.bfloat16)
    pre = jnp.dot(w_self.T, node_feats, preferred_element_type=jnp.float32) + jnp.dot(w_neigh.T, neigh, preferred_element_type=jnp.float32)
    hidden = jnp.maximum(pre, 0.0)
    mean_square = lax.optimization_barrier(jnp.mean(hidden * hidden, axis=0, keepdims=True))
    return (hidden * lax.rsqrt(mean_square + 1e-05)).astype(jnp.bfloat16)
```

```python
import functools

import jax
import jax.numpy as jnp
from jax import lax
from jax.experimental import pallas as pl
from jax.experimental.pallas import tpu as pltpu
from jax.sharding import PartitionSpec as P

MESH = pl.DeviceIdType.MESH
CHUNKS = 4


def kernel(
    chips, groups, chunks,
    feats, tiles_hbm, w_self_hbm, w_neigh_hbm, rows, cols, counts, degree,
    out,
    *scratch,
):
    columns = scratch[:chunks]
    (
        tiles, w_self, w_neigh, w_neigh_t, pre, own, mate_out, mate_in, chain_out, from_low, from_high,
        local_sem, own_sem, gather_send, gather_recv, mate_send, mate_recv,
        chain_send, low_recv, high_recv,
    ) = scratch[chunks:]
    position = lax.axis_index("loop")
    g = lax.axis_index("grp")
    z, core = position // 2, position % 2
    features, nodes = feats.shape
    part = features // chunks
    slots, edge = tiles.shape[1], tiles.shape[2]
    per = nodes // edge

    copies = [
        pltpu.make_async_copy(tiles_hbm, tiles, local_sem.at[0]),
        pltpu.make_async_copy(w_self_hbm, w_self, local_sem.at[1]),
        pltpu.make_async_copy(w_neigh_hbm, w_neigh, local_sem.at[2]),
    ]

    def own_copy(q, r):
        return pltpu.make_async_copy(
            feats.at[pl.ds(q * part, part), pl.ds(r * edge, edge)],
            columns[q].at[g * per + r],
            own_sem.at[q, r],
        )

    def gather(q, offset, r):
        return pltpu.make_async_remote_copy(
            src_ref=feats.at[pl.ds(q * part, part), pl.ds(r * edge, edge)],
            dst_ref=columns[q].at[g * per + r],
            send_sem=gather_send.at[q, offset - 1, r],
            recv_sem=gather_recv.at[q, offset - 1, r],
            device_id={"grp": lax.rem(g + offset, groups)},
            device_id_type=MESH,
        )

    def mate_copy(q, zt):
        return pltpu.make_async_remote_copy(
            src_ref=mate_out.at[zt, q],
            dst_ref=mate_in.at[zt, q],
            send_sem=mate_send.at[zt, q],
            recv_sem=mate_recv.at[zt, q],
            device_id={"loop": z * 2 + 1 - core},
            device_id_type=MESH,
        )

    def up_copy(q, zt):
        return pltpu.make_async_remote_copy(
            src_ref=chain_out.at[zt, q],
            dst_ref=from_low.at[zt, q],
            send_sem=chain_send.at[zt, q],
            recv_sem=low_recv.at[zt, q],
            device_id={"loop": position + 2},
            device_id_type=MESH,
        )

    def down_copy(q, zt):
        return pltpu.make_async_remote_copy(
            src_ref=chain_out.at[zt, q],
            dst_ref=from_high.at[zt, q],
            send_sem=chain_send.at[zt, q],
            recv_sem=high_recv.at[zt, q],
            device_id={"loop": position - 2},
            device_id_type=MESH,
        )

    for q in range(chunks):
        for r in range(per):
            own_copy(q, r).start()
    for copy in copies:
        copy.start()

    barrier = pltpu.get_barrier_semaphore()
    for offset in range(1, groups):
        pl.semaphore_signal(
            barrier, inc=1, device_id={"grp": lax.rem(g + offset, groups)}, device_id_type=MESH
        )
    pl.semaphore_signal(
        barrier, inc=1, device_id={"loop": z * 2 + 1 - core}, device_id_type=MESH
    )

    @pl.when(z > 0)
    def _():
        pl.semaphore_signal(
            barrier, inc=1, device_id={"loop": position - 2}, device_id_type=MESH
        )

    @pl.when(z < chips - 1)
    def _():
        pl.semaphore_signal(
            barrier, inc=1, device_id={"loop": position + 2}, device_id_type=MESH
        )

    inner = jnp.where((z > 0) & (z < chips - 1), 1, 0)
    pl.semaphore_wait(barrier, groups + 1 + inner)

    for q in range(chunks):
        for offset in range(1, groups):
            for r in range(per):
                gather(q, offset, r).start()

    def masked(t, k):
        tile = tiles[t, k]
        block = rows[t, k] - g * per
        live = (k < counts[0, t]).astype(jnp.int32)
        return jnp.concatenate(
            [
                tile * ((block == r).astype(jnp.int32) * live).astype(jnp.float32).astype(tile.dtype)
                for r in range(per)
            ],
            axis=0,
        )

    def picked(q, t, k):
        return columns[q][cols[t, k]]

    def partial(q, t):
        total = None
        for k in range(0, slots, 2):
            pair = range(k, min(k + 2, slots))
            left = jnp.concatenate([picked(q, t, s) for s in pair], axis=1)
            right = jnp.concatenate([masked(t, s) for s in pair], axis=1)
            term = lax.dot_general(
                left, right, (((1,), (1,)), ((), ())), preferred_element_type=jnp.float32
            )
            total = term if total is None else total + term
        return total

    upward = 2 * z < chips

    def target_at(i):
        return jnp.where(upward, chips - 1 - i, i)

    def mate_step(q, i):
        zt = target_at(i)
        mate_out[zt, q] = partial(q, zt * 2 + 1 - core)
        mate_copy(q, zt).start()

    def compute(q):
        for offset in range(1, groups):
            for r in range(per):
                gather(q, offset, r).wait_recv()
        if q == 0:
            for r in range(per):
                own_copy(q, r).wait()
            copies[0].wait()
        mate_step(q, 0)

        @pl.loop(0, chips)
        def _(i):
            @pl.when(i + 1 < chips)
            def _():
                mate_step(q, i + 1)

            zt = target_at(i)
            mine = partial(q, zt * 2 + core)
            mate_copy(q, zt).wait_recv()
            mine = mine + mate_in[zt, q]
            own[zt, q] = mine

            @pl.when((z == 0) & (zt > 0))
            def _():
                chain_out[zt, q] = mine.astype(chain_out.dtype)
                up_copy(q, zt).start()

            @pl.when((z == chips - 1) & (zt < chips - 1))
            def _():
                chain_out[zt, q] = mine.astype(chain_out.dtype)
                down_copy(q, zt).start()

    def relay(q):
        @pl.loop(0, chips - 1)
        def _(d):
            high = chips - 1 - d

            @pl.when((z > 0) & (high > z))
            def _():
                up_copy(q, high).wait_recv()
                chain_out[high, q] = (
                    own[high, q] + from_low[high, q].astype(jnp.float32)
                ).astype(chain_out.dtype)
                up_copy(q, high).start()

            @pl.when((z < chips - 1) & (d < z))
            def _():
                down_copy(q, d).wait_recv()
                chain_out[d, q] = (
                    own[d, q] + from_high[d, q].astype(jnp.float32)
                ).astype(chain_out.dtype)
                down_copy(q, d).start()

        @pl.when(z > 0)
        def _():
            up_copy(q, z).wait_recv()
            own[z, q] += from_low[z, q].astype(jnp.float32)

        @pl.when(z < chips - 1)
        def _():
            down_copy(q, z).wait_recv()
            own[z, q] += from_high[z, q].astype(jnp.float32)

        start = pl.multiple_of(g * nodes, nodes)
        norm = degree[:, pl.ds(start, nodes)].astype(jnp.float32)
        neighbor = (own[z, q] / norm).astype(jnp.bfloat16)
        pre[...] += jnp.dot(
            w_neigh_t[:, q * part:(q + 1) * part], neighbor, preferred_element_type=jnp.float32
        )

    for q in range(chunks):
        compute(q)
        if q == 0:
            copies[1].wait()
            copies[2].wait()
            for later in range(1, chunks):
                for r in range(per):
                    own_copy(later, r).wait()
            w_neigh_t[...] = w_neigh[...].T
            total = None
            for piece in range(chunks):
                term = lax.dot_general(
                    w_self[piece * part:(piece + 1) * part, :],
                    jnp.concatenate([columns[piece][g * per + r] for r in range(per)], axis=1),
                    (((0,), (0,)), ((), ())),
                    preferred_element_type=jnp.float32,
                )
                total = term if total is None else total + term
            pre[...] = total
        else:
            relay(q - 1)
    relay(chunks - 1)

    hidden = jnp.maximum(pre[...], 0.0)
    mean_square = jnp.mean(hidden * hidden, axis=0, keepdims=True)
    out[...] = (hidden * lax.rsqrt(mean_square + 1e-05)).astype(out.dtype)

    for q in range(chunks):
        for offset in range(1, groups):
            for r in range(per):
                gather(q, offset, r).wait_send()

        @pl.loop(0, chips)
        def _(zt):
            mate_copy(q, zt).wait_send()

            @pl.when(zt != z)
            def _():
                up_copy(q, zt).wait_send()


def shards(node_feats, tile_vals, tile_rows, tile_cols, tile_count, degree, w_self, w_neigh):
    loop, groups = lax.axis_size("loop"), lax.axis_size("grp")
    chips = loop // 2
    features, nodes = node_feats.shape
    outputs = w_self.shape[1]
    slots, edge = tile_vals.shape[2], tile_vals.shape[3]
    per = nodes // edge
    chunks = CHUNKS
    part = features // chunks
    piece = (chips, chunks, part, nodes)
    dma = pltpu.SemaphoreType.DMA
    anywhere = pl.BlockSpec(memory_space=pl.ANY)
    scalars = pl.BlockSpec(memory_space=pltpu.SMEM)
    vector = pl.BlockSpec(memory_space=pltpu.VMEM)
    return pl.pallas_call(
        functools.partial(kernel, chips, groups, chunks),
        out_shape=jax.ShapeDtypeStruct((outputs, nodes), jnp.bfloat16),
        in_specs=[anywhere] * 4 + [scalars] * 3 + [vector],
        out_specs=vector,
        scratch_shapes=[pltpu.VMEM((groups * per, part, edge), jnp.bfloat16)] * chunks
        + [
            pltpu.VMEM((loop, slots, edge, edge), jnp.bfloat16),
            pltpu.VMEM(w_self.shape, jnp.bfloat16),
            pltpu.VMEM(w_neigh.shape, jnp.bfloat16),
            pltpu.VMEM((outputs, features), jnp.bfloat16),
            pltpu.VMEM((outputs, nodes), jnp.float32),
            pltpu.VMEM(piece, jnp.float32),
            pltpu.VMEM(piece, jnp.float32),
            pltpu.VMEM(piece, jnp.float32),
            pltpu.VMEM(piece, jnp.bfloat16),
            pltpu.VMEM(piece, jnp.bfloat16),
            pltpu.VMEM(piece, jnp.bfloat16),
            dma((3,)),
            dma((chunks, per)),
            dma((chunks, groups - 1, per)),
            dma((chunks, groups - 1, per)),
            dma((chips, chunks)),
            dma((chips, chunks)),
            dma((chips, chunks)),
            dma((chips, chunks)),
            dma((chips, chunks)),
        ],
        compiler_params=pltpu.CompilerParams(
            collective_id=0, has_side_effects=True, vmem_limit_bytes=60 * 2**20
        ),
    )(
        node_feats,
        tile_vals.reshape(tile_vals.shape[1:]),
        w_self,
        w_neigh,
        tile_rows.reshape(tile_rows.shape[1:]),
        tile_cols.reshape(tile_cols.shape[1:]),
        tile_count,
        degree.reshape(1, -1),
    )


def solution(mesh):
    return jax.shard_map(
        shards,
        mesh=mesh,
        in_specs=(
            P(None, ("loop", "grp")),
            P("loop", None, None, None, None),
            P("loop", None, None),
            P("loop", None, None),
            P("loop", None),
            P("loop"),
            P(),
            P(),
        ),
        out_specs=P(None, ("loop", "grp")),
        check_vma=False,
    )
```

```python
import functools

import jax
import jax.numpy as jnp
from jax import lax
from jax.experimental import pallas as pl
from jax.experimental.pallas import tpu as pltpu
from jax.sharding import PartitionSpec as P

MESH = pl.DeviceIdType.MESH
CHUNKS = 2


def kernel(
    chips, groups, chunks,
    feats, tiles_hbm, w_self_hbm, w_neigh_hbm, rows, cols, counts, degree,
    out,
    *scratch,
):
    columns = scratch[:chunks]
    (
        tiles, w_self, w_neigh, w_neigh_t, pre, own, mate_out, mate_in, chain_out, from_low, from_high,
        local_sem, own_sem, gather_send, gather_recv, mate_send, mate_recv,
        chain_send, low_recv, high_recv,
    ) = scratch[chunks:]
    position = lax.axis_index("loop")
    g = lax.axis_index("grp")
    z, core = position // 2, position % 2
    features, nodes = feats.shape
    part = features // chunks
    slots, edge = tiles.shape[1], tiles.shape[2]
    per = nodes // edge

    copies = [
        pltpu.make_async_copy(tiles_hbm, tiles, local_sem.at[0]),
        pltpu.make_async_copy(w_self_hbm, w_self, local_sem.at[1]),
        pltpu.make_async_copy(w_neigh_hbm, w_neigh, local_sem.at[2]),
    ]

    def own_copy(q, r):
        return pltpu.make_async_copy(
            feats.at[pl.ds(q * part, part), pl.ds(r * edge, edge)],
            columns[q].at[g * per + r],
            own_sem.at[q, r],
        )

    def gather(q, offset, r):
        return pltpu.make_async_remote_copy(
            src_ref=feats.at[pl.ds(q * part, part), pl.ds(r * edge, edge)],
            dst_ref=columns[q].at[g * per + r],
            send_sem=gather_send.at[q, offset - 1, r],
            recv_sem=gather_recv.at[q, offset - 1, r],
            device_id={"grp": lax.rem(g + offset, groups)},
            device_id_type=MESH,
        )

    def mate_copy(q, zt):
        return pltpu.make_async_remote_copy(
            src_ref=mate_out.at[zt, q],
            dst_ref=mate_in.at[zt, q],
            send_sem=mate_send.at[zt, q],
            recv_sem=mate_recv.at[zt, q],
            device_id={"loop": z * 2 + 1 - core},
            device_id_type=MESH,
        )

    def up_copy(q, zt):
        return pltpu.make_async_remote_copy(
            src_ref=chain_out.at[zt, q],
            dst_ref=from_low.at[zt, q],
            send_sem=chain_send.at[zt, q],
            recv_sem=low_recv.at[zt, q],
            device_id={"loop": position + 2},
            device_id_type=MESH,
        )

    def down_copy(q, zt):
        return pltpu.make_async_remote_copy(
            src_ref=chain_out.at[zt, q],
            dst_ref=from_high.at[zt, q],
            send_sem=chain_send.at[zt, q],
            recv_sem=high_recv.at[zt, q],
            device_id={"loop": position - 2},
            device_id_type=MESH,
        )

    for q in range(chunks):
        for r in range(per):
            own_copy(q, r).start()
    for copy in copies:
        copy.start()

    barrier = pltpu.get_barrier_semaphore()
    for offset in range(1, groups):
        pl.semaphore_signal(
            barrier, inc=1, device_id={"grp": lax.rem(g + offset, groups)}, device_id_type=MESH
        )
    pl.semaphore_signal(
        barrier, inc=1, device_id={"loop": z * 2 + 1 - core}, device_id_type=MESH
    )

    @pl.when(z > 0)
    def _():
        pl.semaphore_signal(
            barrier, inc=1, device_id={"loop": position - 2}, device_id_type=MESH
        )

    @pl.when(z < chips - 1)
    def _():
        pl.semaphore_signal(
            barrier, inc=1, device_id={"loop": position + 2}, device_id_type=MESH
        )

    inner = jnp.where((z > 0) & (z < chips - 1), 1, 0)
    pl.semaphore_wait(barrier, groups + 1 + inner)

    def gather_start(q):
        for offset in range(1, groups):
            for r in range(per):
                gather(q, offset, r).start()

    gather_start(0)

    def masked(t, k):
        tile = tiles[t, k]
        block = rows[t, k] - g * per
        live = (k < counts[0, t]).astype(jnp.int32)
        return jnp.concatenate(
            [
                tile * ((block == r).astype(jnp.int32) * live).astype(jnp.float32).astype(tile.dtype)
                for r in range(per)
            ],
            axis=0,
        )

    def picked(q, t, k):
        return columns[q][cols[t, k]]

    def partial(q, t):
        total = None
        for k in range(0, slots, 2):
            pair = range(k, min(k + 2, slots))
            left = jnp.concatenate([picked(q, t, s) for s in pair], axis=1)
            right = jnp.concatenate([masked(t, s) for s in pair], axis=1)
            term = lax.dot_general(
                left, right, (((1,), (1,)), ((), ())), preferred_element_type=jnp.float32
            )
            total = term if total is None else total + term
        return total

    upward = 2 * z < chips
    outer = (z == 0) | (z == chips - 1)

    def target_at(i):
        return jnp.where(upward, chips - 1 - i, i)

    def mate_step(q, i):
        zt = target_at(i)
        mate_out[zt, q] = partial(q, zt * 2 + 1 - core)
        mate_copy(q, zt).start()

    def compute(q):
        for offset in range(1, groups):
            for r in range(per):
                gather(q, offset, r).wait_recv()
        if q + 1 < chunks:
            gather_start(q + 1)
        if q == 0:
            for r in range(per):
                own_copy(q, r).wait()
            copies[0].wait()
        mate_step(q, 0)

        @pl.loop(0, chips)
        def _(i):
            @pl.when(i + 1 < chips)
            def _():
                mate_step(q, i + 1)

            zt = target_at(i)
            mine = partial(q, zt * 2 + core)
            mate_copy(q, zt).wait_recv()
            mine = mine + mate_in[zt, q]
            own[zt, q] = mine

            @pl.when(outer & (i < chips - 1))
            def _():
                chain_out[zt, q] = mine.astype(chain_out.dtype)

                @pl.when(z == 0)
                def _():
                    up_copy(q, zt).start()

                @pl.when(z > 0)
                def _():
                    down_copy(q, zt).start()

    def relay(stage):
        up_q, down_q = stage + 1 - z, stage + 2 + z - chips
        up_live = (z > 0) & (up_q >= 0) & (up_q < chunks)
        down_live = (z < chips - 1) & (down_q >= 0) & (down_q < chunks)

        @pl.loop(0, chips - 1)
        def _(d):
            high = chips - 1 - d

            @pl.when(up_live & (high > z))
            def _():
                up_copy(up_q, high).wait_recv()
                chain_out[high, up_q] = (
                    own[high, up_q] + from_low[high, up_q].astype(jnp.float32)
                ).astype(chain_out.dtype)
                up_copy(up_q, high).start()

            @pl.when(down_live & (d < z))
            def _():
                down_copy(down_q, d).wait_recv()
                chain_out[d, down_q] = (
                    own[d, down_q] + from_high[d, down_q].astype(jnp.float32)
                ).astype(chain_out.dtype)
                down_copy(down_q, d).start()

    def finish(q):
        @pl.when(z > 0)
        def _():
            up_copy(q, z).wait_recv()
            own[z, q] += from_low[z, q].astype(jnp.float32)

        @pl.when(z < chips - 1)
        def _():
            down_copy(q, z).wait_recv()
            own[z, q] += from_high[z, q].astype(jnp.float32)

        start = pl.multiple_of(g * nodes, nodes)
        norm = degree[:, pl.ds(start, nodes)].astype(jnp.float32)
        neighbor = (own[z, q] / norm).astype(jnp.bfloat16)
        pre[...] += jnp.dot(
            w_neigh_t[:, q * part:(q + 1) * part], neighbor, preferred_element_type=jnp.float32
        )

    for q in range(chunks):
        compute(q)
        if q == 0:
            copies[1].wait()
            copies[2].wait()
            for later in range(1, chunks):
                for r in range(per):
                    own_copy(later, r).wait()
            w_neigh_t[...] = w_neigh[...].T
            total = None
            for piece in range(chunks):
                term = lax.dot_general(
                    w_self[piece * part:(piece + 1) * part, :],
                    jnp.concatenate([columns[piece][g * per + r] for r in range(per)], axis=1),
                    (((0,), (0,)), ((), ())),
                    preferred_element_type=jnp.float32,
                )
                total = term if total is None else total + term
            pre[...] = total
        relay(q)
    for stage in range(chunks, chunks + max(chips - 3, 0)):
        relay(stage)
    for q in range(chunks):
        finish(q)

    hidden = jnp.maximum(pre[...], 0.0)
    mean_square = jnp.mean(hidden * hidden, axis=0, keepdims=True)
    out[...] = (hidden * lax.rsqrt(mean_square + 1e-05)).astype(out.dtype)

    for q in range(chunks):
        for offset in range(1, groups):
            for r in range(per):
                gather(q, offset, r).wait_send()

        @pl.loop(0, chips)
        def _(zt):
            mate_copy(q, zt).wait_send()

            @pl.when(zt != z)
            def _():
                up_copy(q, zt).wait_send()


def shards(node_feats, tile_vals, tile_rows, tile_cols, tile_count, degree, w_self, w_neigh):
    loop, groups = lax.axis_size("loop"), lax.axis_size("grp")
    chips = loop // 2
    features, nodes = node_feats.shape
    outputs = w_self.shape[1]
    slots, edge = tile_vals.shape[2], tile_vals.shape[3]
    per = nodes // edge
    chunks = CHUNKS
    part = features // chunks
    piece = (chips, chunks, part, nodes)
    dma = pltpu.SemaphoreType.DMA
    anywhere = pl.BlockSpec(memory_space=pl.ANY)
    scalars = pl.BlockSpec(memory_space=pltpu.SMEM)
    vector = pl.BlockSpec(memory_space=pltpu.VMEM)
    return pl.pallas_call(
        functools.partial(kernel, chips, groups, chunks),
        out_shape=jax.ShapeDtypeStruct((outputs, nodes), jnp.bfloat16),
        in_specs=[anywhere] * 4 + [scalars] * 3 + [vector],
        out_specs=vector,
        scratch_shapes=[pltpu.VMEM((groups * per, part, edge), jnp.bfloat16)] * chunks
        + [
            pltpu.VMEM((loop, slots, edge, edge), jnp.bfloat16),
            pltpu.VMEM(w_self.shape, jnp.bfloat16),
            pltpu.VMEM(w_neigh.shape, jnp.bfloat16),
            pltpu.VMEM((outputs, features), jnp.bfloat16),
            pltpu.VMEM((outputs, nodes), jnp.float32),
            pltpu.VMEM(piece, jnp.float32),
            pltpu.VMEM(piece, jnp.float32),
            pltpu.VMEM(piece, jnp.float32),
            pltpu.VMEM(piece, jnp.bfloat16),
            pltpu.VMEM(piece, jnp.bfloat16),
            pltpu.VMEM(piece, jnp.bfloat16),
            dma((3,)),
            dma((chunks, per)),
            dma((chunks, groups - 1, per)),
            dma((chunks, groups - 1, per)),
            dma((chips, chunks)),
            dma((chips, chunks)),
            dma((chips, chunks)),
            dma((chips, chunks)),
            dma((chips, chunks)),
        ],
        compiler_params=pltpu.CompilerParams(
            collective_id=0, has_side_effects=True, vmem_limit_bytes=60 * 2**20
        ),
    )(
        node_feats,
        tile_vals.reshape(tile_vals.shape[1:]),
        w_self,
        w_neigh,
        tile_rows.reshape(tile_rows.shape[1:]),
        tile_cols.reshape(tile_cols.shape[1:]),
        tile_count,
        degree.reshape(1, -1),
    )


def solution(mesh):
    return jax.shard_map(
        shards,
        mesh=mesh,
        in_specs=(
            P(None, ("loop", "grp")),
            P("loop", None, None, None, None),
            P("loop", None, None),
            P("loop", None, None),
            P("loop", None),
            P("loop"),
            P(),
            P(),
        ),
        out_specs=P(None, ("loop", "grp")),
        check_vma=False,
    )
```
